32 devices in a mesh: row: 4 (over y, core), col: 8 (over z, x).
Axes of the slice: x: 2, y: 2, z: 4, core: 2. Of those that a mesh axis runs over, the one named last changes fastest.
Arguments:
- start_vecs: bfloat16 [32, 1, 4, 8, 512], P(None, None, 'row', 'col'), may hold values from -6 to 6
- blocks: bfloat16 [4, 8, 6, 512, 512], P('row', 'col'), may hold values from -0.125 to 0.125
- block_rows: int32 [4, 8, 6], P('row', 'col'), may hold values from 0 to 3, as said below
- block_cols: int32 [4, 8, 6], P('row', 'col'), may hold values from 0 to 7, as said below
- block_count: int32 [4, 8], P('row', 'col'), may hold values from 3 to 6, as said below
Outputs:
- filtered_one: bfloat16 [32, 1, 4, 8, 512], P(None, None, 'row', 'col')
- filtered_two: bfloat16 [32, 1, 4, 8, 512], P(None, None, 'row', 'col')
The draws below stay inside these ranges and needn't reach their ends.
Inputs may be any that keep to these rules, and one draw needn't show every extreme that they name: `block_rows`: on device (a, b) a slot with value i has block row I = (i // 4) * 4 * 8 + (i % 4) * 8 + b, and I <= J for the slot's block column J; a pair (I, J) may repeat. `block_cols`: on device (a, b) a slot with value j has block column J = (j // 8) * 4 * 8 + a * 8 + j % 8. The used slots are the first block_count[a, b] of each device; the others are ignored; some device uses all 6.
All inputs are finite; a program needn't handle non-finite values.
Results may differ from the reference program's by a relative error of at most 0.015.
Values may be sent and summed in bfloat16 or wider, within the bound.
No kernel may reach another device: no remote copies, remote signals or barrier semaphores. Data moves between devices by JAX's collectives and lax.ppermute only.
A program may use at most 64 MiB of HBM per device.

```python
import jax
import jax.numpy as jnp
from jax import lax

BS = 512
NV = 32
NBD = 1
SLOTS = 6
STEPS = 2
N_ROW = 4
N_COL = 8


def pattern(key):
    key_list = jax.random.split(key, 8)
    slot_shape = (N_ROW, N_COL, SLOTS)
    row_owner = jnp.arange(N_ROW, dtype=jnp.int32)[:, None, None]
    col_owner = jnp.arange(N_COL, dtype=jnp.int32)[None, :, None]
    row_round = jax.random.randint(key_list[0], slot_shape, 0, NBD, dtype=jnp.int32)
    row_group = jax.random.randint(key_list[1], slot_shape, 0, N_ROW, dtype=jnp.int32)
    col_round = jax.random.randint(key_list[2], slot_shape, 0, NBD, dtype=jnp.int32)
    col_group = jax.random.randint(key_list[3], slot_shape, 0, N_COL, dtype=jnp.int32)
    grid_size = N_ROW * N_COL
    block_row = row_round * grid_size + row_group * N_COL + col_owner
    block_col = col_round * grid_size + row_owner * N_COL + col_group
    diag_round = jax.random.randint(key_list[4], slot_shape, 0, NBD, dtype=jnp.int32)
    is_upper = block_row <= block_col
    local_rows = jnp.where(is_upper, row_round * N_ROW + row_group, diag_round * N_ROW + row_owner)
    local_cols = jnp.where(is_upper, col_round * N_COL + col_group, diag_round * N_COL + col_owner)
    missing = jax.random.randint(key_list[5], (N_ROW, N_COL), 0, SLOTS // 2 + 1, dtype=jnp.int32)
    counts = SLOTS - missing
    busiest = jax.random.randint(key_list[7], (), 0, grid_size, dtype=jnp.int32)
    device_ids = jnp.arange(grid_size, dtype=jnp.int32).reshape(N_ROW, N_COL)
    counts = jnp.where(device_ids == busiest, SLOTS, counts).astype(jnp.int32)
    return (local_rows.astype(jnp.int32), local_cols.astype(jnp.int32), counts)


def draw_block_rows(key, part):
    shared = pattern(key)
    return shared[0]


def draw_block_cols(key, part):
    shared = pattern(key)
    return shared[1]


def draw_block_count(key, part):
    shared = pattern(key)
    return shared[2]


def levels(own_key, dims, cuts, smallest, largest):
    factor_of = 1.0
    for position, blocks in cuts:
        steps = jax.random.uniform(jax.random.fold_in(jax.random.fold_in(own_key, 6), position), (blocks,), jnp.float32, smallest / len(cuts), largest / len(cuts))
        factor_of = factor_of * jnp.repeat(jnp.exp(steps), dims[position] // blocks).reshape((-1,) + (1,) * (len(dims) - 1 - position))
    return factor_of


def noise(key, extent, width, reach, cuts=(), kind=jnp.bfloat16):
    loudness = levels(key, extent, cuts, -0.22, 0.18) if cuts else 1.0
    array = jax.random.normal(key, extent, jnp.float32) * width * loudness
    return jnp.minimum(jnp.maximum(array, -reach), reach).astype(kind)


def setup_inputs(seed: int = 0) -> dict:
    streams_of = jax.random.split(jax.random.key(seed), 6)
    return {
        "start_vecs": noise(streams_of[0], (NV, NBD, N_ROW, N_COL, BS), 1.0, 6.0, ((2, 4), (3, 8))),
        "blocks": noise(streams_of[1], (N_ROW, N_COL, SLOTS, BS, BS), (BS * (SLOTS // 2 + 1)) ** -0.5, 0.125, ((0, 4), (1, 8))),
        "block_rows": draw_block_rows(jax.random.fold_in(streams_of[5], 71), 0),
        "block_cols": draw_block_cols(jax.random.fold_in(streams_of[5], 71), 0),
        "block_count": draw_block_count(jax.random.fold_in(streams_of[5], 71), 0),
    }


shift_center = 0.5
half_width = 2.0


def settle(values):
    return lax.optimization_barrier(values.astype(jnp.bfloat16)).astype(jnp.float32)


def add_block(running, index_at, product):
    before = lax.dynamic_index_in_dim(running, index_at, 1, keepdims=False)
    return lax.dynamic_update_index_in_dim(running, before + product, index_at, 1)


def apply_matrix(vectors, blocks, block_rows, block_cols, block_count):
    vec_count = vectors.shape[0]
    device_total = N_ROW * N_COL
    tile_stack = blocks.reshape(device_total, SLOTS, BS, BS)
    row_lists = block_rows.reshape(device_total, SLOTS)
    col_lists = block_cols.reshape(device_total, SLOTS)
    live_counts = block_count.reshape(device_total)
    device_ids = jnp.arange(device_total, dtype=jnp.int32)

    def device_step(running, device_item):
        device_id, row_list, col_list, live_count, tiles_here = device_item
        owner_row = device_id // N_COL
        owner_col = device_id % N_COL
        owner_vecs = lax.dynamic_index_in_dim(vectors, owner_col, 3, keepdims=False).reshape(vec_count, NBD * N_ROW, BS)
        mirror_vecs = lax.dynamic_index_in_dim(vectors, owner_row, 2, keepdims=False).reshape(vec_count, NBD * N_COL, BS)

        def slot_step(slot_at, partials):
            direct, mirror = partials
            block_tile = lax.dynamic_index_in_dim(tiles_here, slot_at, 0, keepdims=False)
            row_at = row_list[slot_at]
            col_at = col_list[slot_at]
            source = lax.dynamic_index_in_dim(mirror_vecs, col_at, 1, keepdims=False)
            direct = add_block(direct, row_at, lax.dot_general(source, block_tile, (((1,), (1,)), ((), ())), preferred_element_type=jnp.float32))
            source = lax.dynamic_index_in_dim(owner_vecs, row_at, 1, keepdims=False)
            mirror = add_block(mirror, col_at, jnp.dot(source, block_tile, preferred_element_type=jnp.float32))
            return direct, mirror

        initial = (jnp.zeros((vec_count, NBD * N_ROW, BS), jnp.float32), jnp.zeros((vec_count, NBD * N_COL, BS), jnp.float32))
        direct, mirror = lax.fori_loop(0, live_count, slot_step, initial)
        direct = settle(direct).reshape(vec_count, NBD, N_ROW, 1, BS)
        mirror = settle(mirror).reshape(vec_count, NBD, 1, N_COL, BS)
        anchor = jnp.zeros((), jnp.int32)
        start_one = (anchor, anchor, anchor, owner_col, anchor)
        before = lax.dynamic_slice(running, start_one, direct.shape)
        running = lax.dynamic_update_slice(running, before + direct, start_one)
        start_two = (anchor, anchor, owner_row, anchor, anchor)
        before = lax.dynamic_slice(running, start_two, mirror.shape)
        running = lax.dynamic_update_slice(running, before + mirror, start_two)
        return running, None

    running = jnp.zeros(vectors.shape, jnp.float32)
    running, unused = lax.scan(device_step, running, (device_ids, row_lists, col_lists, live_counts, tile_stack))
    return running


def advance(applied, current, previous, section_at):
    shifted = (applied - shift_center * current.astype(jnp.float32)) / half_width
    if section_at > 0:
        shifted = 2.0 * shifted - previous.astype(jnp.float32)
    return shifted.astype(jnp.bfloat16)


def reference(start_vecs, blocks, block_rows, block_cols, block_count):
    previous = start_vecs
    current = start_vecs
    first_result = start_vecs
    for section_at in range(STEPS):
        applied = apply_matrix(current, blocks, block_rows, block_cols, block_count)
        updated = advance(applied, current, previous, section_at)
        if section_at == 0:
            first_result = updated
        previous = current
        current = updated
    return first_result, current
```

```python
import jax
import jax.numpy as jnp
from jax import lax
from jax.experimental import pallas as pl
from jax.experimental.pallas import tpu as pltpu
from jax.sharding import PartitionSpec as P

shift_center = 0.5
half_width = 2.0

VMEM = pl.BlockSpec(memory_space=pltpu.VMEM)
SMEM = pl.BlockSpec(memory_space=pltpu.SMEM)
PARAMS = pltpu.CompilerParams(vmem_limit_bytes=16 * 1024 * 1024)
f32 = jnp.float32
bf16 = jnp.bfloat16


def swap(value, axes, pattern):
    if isinstance(axes, str):
        pairs = [(i, i ^ pattern) for i in range(lax.axis_size(axes))]
    else:
        n_first, n_second = (lax.axis_size(a) for a in axes)
        pairs = [
            (i * n_second + j, (i ^ pattern[0]) * n_second + (j ^ pattern[1]))
            for i in range(n_first)
            for j in range(n_second)
        ]
    return lax.ppermute(value, axes, pairs)


def spread(values, axis):
    pair = jnp.concatenate(values, axis=0)
    return [pair] + [swap(pair, axis, s << 1) for s in range(1, lax.axis_size(axis) // 2)]


def slot_products(meta, tiles, row_pairs, col_pairs):
    slots, width = tiles.shape[0], tiles.shape[1]
    n_vec = row_pairs[0].shape[0] // 2
    n_row, n_col = len(row_pairs), len(col_pairs)

    def kernel(meta_ref, tiles_ref, *refs):
        row_in, refs = refs[:n_row], refs[n_row:]
        col_in, refs = refs[:n_col], refs[n_col:]
        row_out, refs = refs[:n_row], refs[n_row:]
        col_out, refs = refs[:n_col], refs[n_col:]
        row_vecs, col_vecs, direct, mirror = refs
        for source, panel in ((row_in, row_vecs), (col_in, col_vecs)):
            for k, ref in enumerate(source):
                for half in range(2):
                    panel[2 * k + half] = ref[half * n_vec : (half + 1) * n_vec, :]
        direct[...] = jnp.zeros(direct.shape, f32)
        mirror[...] = jnp.zeros(mirror.shape, f32)
        count = meta_ref[2 * slots]
        for s in range(slots):
            used = s < count
            r = meta_ref[s]
            c = meta_ref[slots + s]
            tile = tiles_ref[s]
            source = jnp.where(used, col_vecs[c], jnp.zeros((), bf16))
            owner = lax.dot_general(source, tile, (((1,), (1,)), ((), ())), preferred_element_type=f32)
            source = jnp.where(used, row_vecs[r], jnp.zeros((), bf16))
            other = jnp.dot(source, tile, preferred_element_type=f32)
            direct[r] += owner
            mirror[c] += other
        for total, outs in ((direct, row_out), (mirror, col_out)):
            for k, ref in enumerate(outs):
                for half in range(2):
                    ref[half * n_vec : (half + 1) * n_vec, :] = total[2 * k + half].astype(ref.dtype)

    def outs(n):
        return [jax.ShapeDtypeStruct((2 * n_vec, width), f32 if k == 0 else bf16) for k in range(n)]

    done = pl.pallas_call(
        kernel,
        out_shape=outs(n_row) + outs(n_col),
        in_specs=[SMEM, VMEM] + [VMEM] * (n_row + n_col),
        out_specs=[VMEM] * (n_row + n_col),
        scratch_shapes=[
            pltpu.VMEM((2 * n_row, n_vec, width), bf16),
            pltpu.VMEM((2 * n_col, n_vec, width), bf16),
            pltpu.VMEM((2 * n_row, n_vec, width), f32),
            pltpu.VMEM((2 * n_col, n_vec, width), f32),
        ],
        compiler_params=PARAMS,
        cost_estimate=pl.CostEstimate(
            flops=slots * 4 * n_vec * width * width, bytes_accessed=slots * width * width * 2, transcendentals=0
        ),
    )(meta, tiles, *row_pairs, *col_pairs)
    return done[:n_row], done[n_row:]


def local_call(kernel, shapes, *operands):
    return pl.pallas_call(
        kernel,
        out_shape=[jax.ShapeDtypeStruct(s, d) for s, d in shapes],
        in_specs=[VMEM] * len(operands),
        out_specs=[VMEM] * len(shapes),
        compiler_params=PARAMS,
    )(*operands)


def scatter_high(terms, axis):
    return [swap(t, axis, s << 1) for s, t in enumerate(terms) if s > 0]


def total_of(kept, received, half, n_vec):
    rows = slice(half * n_vec, (half + 1) * n_vec)
    total = kept[rows, :]
    for ref in received:
        total = total + ref[rows, :].astype(f32)
    return total


def body(start_vecs, blocks, block_rows, block_cols, block_count):
    n_vec, width = start_vecs.shape[0], start_vecs.shape[4]
    tiles = blocks[0, 0]
    slots = tiles.shape[0]
    row_at, col_at = lax.axis_index("row"), lax.axis_index("col")
    count = block_count[0, 0]
    live = jnp.arange(slots, dtype=jnp.int32) < count
    meta = jnp.concatenate(
        [
            jnp.where(live, block_rows[0, 0] ^ row_at, 0),
            jnp.where(live, block_cols[0, 0] ^ col_at, 0),
            count[None],
        ]
    )
    current = start_vecs.reshape(n_vec, width)
    one, two = (n_vec, width), (2 * n_vec, width)

    by_x = swap(current, "col", 1)
    by_core = swap(current, "row", 1)
    row_pairs = spread([current, by_core], "row")
    col_pairs = spread([current, by_x], "col")

    direct, mirror = slot_products(meta, tiles, row_pairs, col_pairs)
    direct_in = scatter_high(direct, "row")
    mirror_in = scatter_high(mirror, "col")
    n_d, n_m = len(direct_in), len(mirror_in)

    def partial_sums(d_ref, m_ref, *refs):
        d_in, m_in, outs = refs[:n_d], refs[n_d : n_d + n_m], refs[n_d + n_m :]
        d_keep, m_keep, to_core, to_x, to_diag = outs
        d = [total_of(d_ref, d_in, half, n_vec) for half in range(2)]
        m = [total_of(m_ref, m_in, half, n_vec) for half in range(2)]
        both = (d[0] + m[0]).astype(bf16)
        low, high = slice(0, n_vec), slice(n_vec, 2 * n_vec)
        for half, rows in enumerate((low, high)):
            d_keep[rows, :] = d[half]
            m_keep[rows, :] = m[half]
        d_1, m_1 = d[1].astype(bf16), m[1].astype(bf16)
        to_core[low, :] = d_1
        to_core[high, :] = both
        to_x[low, :] = m_1
        to_x[high, :] = both
        to_diag[low, :] = d_1
        to_diag[high, :] = m_1

    d_keep, m_keep, to_core, to_x, to_diag = local_call(
        partial_sums,
        [(two, f32), (two, f32), (two, bf16), (two, bf16), (two, bf16)],
        direct[0], mirror[0], *direct_in, *mirror_in,
    )
    from_x = swap(to_x, "col", 1)
    from_diag = swap(to_diag, ("row", "col"), (1, 1))
    from_core = swap(to_core, "row", 1)

    def first_update(d_ref, m_ref, core_ref, x_ref, diag_ref, cur_ref, cur_core, cur_x, own_out, row_out, col_out):
        low, high = slice(0, n_vec), slice(n_vec, 2 * n_vec)

        def get(ref, rows):
            return ref[rows, :].astype(f32)

        def advance(applied, ref):
            shifted = (applied - shift_center * ref[...].astype(f32)) / half_width
            return shifted.astype(bf16)

        own = d_ref[low, :] + m_ref[low, :] + get(core_ref, low) + get(x_ref, low)
        core = d_ref[high, :] + get(core_ref, high) + get(diag_ref, high)
        across = m_ref[high, :] + get(x_ref, high) + get(diag_ref, low)
        own = advance(own, cur_ref)
        own_out[...] = own
        row_out[low, :] = own
        col_out[low, :] = own
        row_out[high, :] = advance(core, cur_core)
        col_out[high, :] = advance(across, cur_x)

    first, row_pair, col_pair = local_call(
        first_update,
        [(one, bf16), (two, bf16), (two, bf16)],
        d_keep, m_keep, from_core, from_x, from_diag, current, by_core, by_x,
    )
    row_pairs = [row_pair] + [swap(row_pair, "row", s << 1) for s in range(1, lax.axis_size("row") // 2)]
    col_pairs = [col_pair] + [swap(col_pair, "col", s << 1) for s in range(1, lax.axis_size("col") // 2)]

    direct, mirror = slot_products(meta, tiles, row_pairs, col_pairs)
    direct_in = scatter_high(direct, "row")
    mirror_in = scatter_high(mirror, "col")

    def last_sums(d_ref, m_ref, *refs):
        d_in, m_in, outs = refs[:n_d], refs[n_d : n_d + n_m], refs[n_d + n_m :]
        keep, to_core, to_x = outs
        keep[...] = total_of(d_ref, d_in, 0, n_vec) + total_of(m_ref, m_in, 0, n_vec)
        to_core[...] = total_of(d_ref, d_in, 1, n_vec).astype(bf16)
        to_x[...] = total_of(m_ref, m_in, 1, n_vec).astype(bf16)

    keep, to_core, to_x = local_call(
        last_sums,
        [(one, f32), (one, bf16), (one, bf16)],
        direct[0], mirror[0], *direct_in, *mirror_in,
    )
    from_x = swap(to_x, "col", 1)
    from_core = swap(to_core, "row", 1)

    def last_update(keep_ref, core_ref, x_ref, cur_ref, prev_ref, out_ref):
        applied = keep_ref[...] + core_ref[...].astype(f32) + x_ref[...].astype(f32)
        shifted = (applied - shift_center * cur_ref[...].astype(f32)) / half_width
        shifted = 2.0 * shifted - prev_ref[...].astype(f32)
        out_ref[...] = shifted.astype(bf16)

    (second,) = local_call(last_update, [(one, bf16)], keep, from_core, from_x, first, current)
    shape = start_vecs.shape
    return first.reshape(shape), second.reshape(shape)


def solution(mesh):
    return jax.shard_map(
        body,
        mesh=mesh,
        in_specs=(
            P(None, None, "row", "col", None),
            P("row", "col", None, None, None),
            P("row", "col", None),
            P("row", "col", None),
            P("row", "col"),
        ),
        out_specs=(P(None, None, "row", "col", None), P(None, None, "row", "col", None)),
        check_vma=False,
    )
```

```python
import jax
import jax.numpy as jnp
from jax import lax
from jax.experimental import pallas as pl
from jax.experimental.pallas import tpu as pltpu
from jax.sharding import PartitionSpec as P

shift_center = 0.5
half_width = 2.0

VMEM = pl.BlockSpec(memory_space=pltpu.VMEM)
SMEM = pl.BlockSpec(memory_space=pltpu.SMEM)
PARAMS = pltpu.CompilerParams(vmem_limit_bytes=16 * 1024 * 1024)
f32 = jnp.float32
bf16 = jnp.bfloat16


def swap(value, axis, pattern):
    return lax.ppermute(value, axis, [(i, i ^ pattern) for i in range(lax.axis_size(axis))])


def local_call(kernel, shapes, *operands, specs=None, scratch=(), flops=1000, nbytes=100000, params=PARAMS):
    return pl.pallas_call(
        kernel,
        out_shape=[jax.ShapeDtypeStruct(s, d) for s, d in shapes],
        in_specs=specs or [VMEM] * len(operands),
        out_specs=[VMEM] * len(shapes),
        scratch_shapes=scratch,
        compiler_params=params,
        cost_estimate=pl.CostEstimate(flops=flops, bytes_accessed=nbytes, transcendentals=0),
    )(*operands)


def prepare(blocks, start_vecs, block_rows, block_cols, block_count):
    slots = blocks.shape[2]

    def kernel(count_ref, rows_hbm, cols_hbm, blocks_hbm, vecs_hbm, tiles_out, vecs_out, meta_out, rows_ref, cols_ref, sems):
        copies = [
            pltpu.make_async_copy(rows_hbm, rows_ref, sems.at[slots + 1]),
            pltpu.make_async_copy(cols_hbm, cols_ref, sems.at[slots + 2]),
        ]
        copies += [pltpu.make_async_copy(vecs_hbm, vecs_out, sems.at[slots])]
        copies += [pltpu.make_async_copy(blocks_hbm.at[0, 0, s], tiles_out.at[s], sems.at[s]) for s in range(slots)]
        for copy in copies:
            copy.start()
        row_at, col_at = lax.axis_index("row"), lax.axis_index("col")
        for copy in copies[:2]:
            copy.wait()
        count = count_ref[0, 0]
        for s in range(slots):
            meta_out[s] = jnp.where(s < count, rows_ref[0, 0, s] ^ row_at, 0)
            meta_out[slots + s] = jnp.where(s < count, cols_ref[0, 0, s] ^ col_at, 0)
        meta_out[2 * slots] = count
        for copy in copies[2:]:
            copy.wait()

    arrays = (block_rows, block_cols, blocks, start_vecs)
    return pl.pallas_call(
        kernel,
        out_shape=[
            pltpu.VMEM(blocks.shape[2:], blocks.dtype),
            pltpu.VMEM(start_vecs.shape, start_vecs.dtype),
            pltpu.SMEM((2 * slots + 1,), jnp.int32),
        ],
        in_specs=[SMEM] + [pl.BlockSpec(memory_space=pltpu.HBM)] * len(arrays),
        out_specs=[VMEM, VMEM, SMEM],
        scratch_shapes=[pltpu.SMEM(a.shape, a.dtype) for a in arrays[:2]] + [pltpu.SemaphoreType.DMA((slots + 3,))],
        compiler_params=PARAMS,
        cost_estimate=pl.CostEstimate(flops=1000, bytes_accessed=2 * blocks.size * 2, transcendentals=0),
    )(block_count, *[pltpu.with_memory_space_constraint(a, pltpu.HBM) for a in arrays])


class Axis:
    def __init__(self, name, bit):
        self.name, self.bit = name, bit
        self.size = lax.axis_size(name)
        self.inner = [i for i in range(self.size) if not i & bit]

    def swap_pair(self, value):
        return swap(value, self.name, self.bit)

    def spread(self, pair):
        return [pair if i == 0 else swap(pair, self.name, i) for i in self.inner]

    def collect(self, terms):
        return [swap(t, self.name, i) for i, t in zip(self.inner, terms, strict=True) if i][::-1]


def slot_products(meta, tiles, pairs, source, target, after=()):
    slots, width = tiles.shape[0], tiles.shape[1]
    n_vec = pairs[0].shape[0] // 2
    n_in, n_out = len(pairs), len(target.inner)
    mirrored = source.name == "row"

    def kernel(meta_ref, tiles_ref, *refs):
        ins, refs = refs[:n_in], refs[n_in + len(after) :]
        outs, (vecs, totals) = refs[:n_out], refs[n_out:]
        for i, ref in zip(source.inner, ins, strict=True):
            for half in range(2):
                vecs[i + half * source.bit] = ref[half * n_vec : (half + 1) * n_vec, :]
        totals[...] = jnp.zeros(totals.shape, f32)
        count = meta_ref[2 * slots]
        for s in range(slots):
            r, c = meta_ref[s], meta_ref[slots + s]
            at, to = (r, c) if mirrored else (c, r)
            values = jnp.where(s < count, vecs[at], jnp.zeros((), bf16))
            product = lax.dot_general(
                values, tiles_ref[s], (((1,), (0 if mirrored else 1,)), ((), ())), preferred_element_type=f32
            )
            totals[to] += product
        for i, ref in zip(target.inner[::-1], outs, strict=True):
            for half in range(2):
                ref[half * n_vec : (half + 1) * n_vec, :] = totals[i + half * target.bit].astype(ref.dtype)

    return local_call(
        kernel,
        [((2 * n_vec, width), f32 if k == n_out - 1 else bf16) for k in range(n_out)],
        meta, tiles, *pairs, *after,
        specs=[SMEM] + [VMEM] * (1 + n_in + len(after)),
        scratch=[pltpu.VMEM((source.size, n_vec, width), bf16), pltpu.VMEM((target.size, n_vec, width), f32)],
        flops=slots * 2 * n_vec * width * width,
        nbytes=slots * width * width * 2,
    )[::-1]


def body(start_vecs, blocks, block_rows, block_cols, block_count):
    n_vec, width = start_vecs.shape[0], start_vecs.shape[4]
    rows_axis = Axis("row", lax.axis_size("row") // 2)
    cols_axis = Axis("col", 1)
    tiles, start_here, meta = prepare(blocks, start_vecs.reshape(n_vec, width), block_rows, block_cols, block_count)
    start = start_vecs.reshape(n_vec, width)
    one, two = (n_vec, width), (2 * n_vec, width)
    low, high = slice(0, n_vec), slice(n_vec, 2 * n_vec)
    n_d, n_m = len(rows_axis.inner), len(cols_axis.inner)

    def products(row_pair, col_pair):
        mirror = slot_products(meta, tiles, rows_axis.spread(row_pair), rows_axis, cols_axis)
        direct = slot_products(meta, tiles, cols_axis.spread(col_pair), cols_axis, rows_axis, mirror[:1])
        return [direct[0], *rows_axis.collect(direct)], [mirror[0], *cols_axis.collect(mirror)]

    def sum_of(refs, rows):
        total = refs[0][rows, :]
        for ref in refs[1:]:
            total = total + ref[rows, :].astype(f32)
        return total

    def get(ref, rows):
        return ref[rows, :].astype(f32)

    start_y, start_x = rows_axis.swap_pair(start), cols_axis.swap_pair(start)

    def join(own_ref, other_ref, out_ref):
        out_ref[low, :] = own_ref[...]
        out_ref[high, :] = other_ref[...]

    (row_pair,) = local_call(join, [(two, bf16)], start_here, start_y)
    (col_pair,) = local_call(join, [(two, bf16)], start_here, start_x)

    d_terms, m_terms = products(row_pair, col_pair)

    def partial_sums(*refs):
        d_in, m_in = refs[:n_d], refs[n_d : n_d + n_m]
        to_diag, to_x, to_y, d_keep, m_keep = refs[n_d + n_m :]
        d_own, d_other = sum_of(d_in, low), sum_of(d_in, high)
        m_own, m_other = sum_of(m_in, low), sum_of(m_in, high)
        d_keep[low, :] = d_own
        d_keep[high, :] = d_other
        m_keep[low, :] = m_own
        m_keep[high, :] = m_other
        both = (d_own + m_own).astype(bf16)
        d_other, m_other = d_other.astype(bf16), m_other.astype(bf16)
        to_y[low, :] = d_other
        to_y[high, :] = both
        to_x[low, :] = m_other
        to_x[high, :] = both
        to_diag[low, :] = d_other
        to_diag[high, :] = m_other

    to_diag, to_x, to_y, d_keep, m_keep = local_call(
        partial_sums,
        [(two, bf16), (two, bf16), (two, bf16), (two, f32), (two, f32)],
        *d_terms, *m_terms,
    )
    n_row, n_col = rows_axis.size, cols_axis.size
    diagonal = [
        (i * n_col + j, (i ^ rows_axis.bit) * n_col + (j ^ cols_axis.bit)) for i in range(n_row) for j in range(n_col)
    ]
    from_diag = lax.ppermute(to_diag, ("row", "col"), diagonal)
    from_x = cols_axis.swap_pair(to_x)
    from_y = rows_axis.swap_pair(to_y)

    def first_update(diag_ref, x_ref, y_ref, d_ref, m_ref, cur, cur_y, cur_x, row_out, col_out):
        def advance(applied, ref):
            shifted = (applied - shift_center * ref[...].astype(f32)) / half_width
            return shifted.astype(bf16)

        own = d_ref[low, :] + m_ref[low, :] + get(y_ref, low) + get(x_ref, low)
        own = advance(own, cur)
        row_out[low, :] = own
        col_out[low, :] = own
        row_out[high, :] = advance(d_ref[high, :] + get(y_ref, high) + get(diag_ref, high), cur_y)
        col_out[high, :] = advance(m_ref[high, :] + get(x_ref, high) + get(diag_ref, low), cur_x)

    row_pair, col_pair = local_call(
        first_update, [(two, bf16), (two, bf16)],
        from_diag, from_x, from_y, d_keep, m_keep, start_here, start_y, start_x,
    )

    d_terms, m_terms = products(row_pair, col_pair)

    def last_sums(*refs):
        d_in, m_in, (keep, to_y, to_x) = refs[:n_d], refs[n_d : n_d + n_m], refs[n_d + n_m :]
        keep[...] = sum_of(d_in, low) + sum_of(m_in, low)
        to_y[...] = sum_of(d_in, high).astype(bf16)
        to_x[...] = sum_of(m_in, high).astype(bf16)

    keep, to_y, to_x = local_call(last_sums, [(one, f32), (one, bf16), (one, bf16)], *d_terms, *m_terms)
    from_x = cols_axis.swap_pair(to_x)
    from_y = rows_axis.swap_pair(to_y)

    def last_update(keep_ref, y_ref, x_ref, pair_ref, prev_ref, first_out, second_out):
        current = pair_ref[low, :]
        applied = keep_ref[...] + y_ref[...].astype(f32) + x_ref[...].astype(f32)
        shifted = (applied - shift_center * current.astype(f32)) / half_width
        shifted = 2.0 * shifted - prev_ref[...].astype(f32)
        first_out[...] = current
        second_out[...] = shifted.astype(bf16)

    first, second = local_call(
        last_update, [(one, bf16), (one, bf16)], keep, from_y, from_x, row_pair, start_here
    )
    shape = start_vecs.shape
    return first.reshape(shape), second.reshape(shape)


def solution(mesh):
    return jax.shard_map(
        body,
        mesh=mesh,
        in_specs=(
            P(None, None, "row", "col", None),
            P("row", "col", None, None, None),
            P("row", "col", None),
            P("row", "col", None),
            P("row", "col"),
        ),
        out_specs=(P(None, None, "row", "col", None), P(None, None, "row", "col", None)),
        check_vma=False,
    )
```

```python
import jax
import jax.numpy as jnp
from jax import lax
from jax.experimental import pallas as pl
from jax.experimental.pallas import tpu as pltpu
from jax.sharding import PartitionSpec as P

shift_center = 0.5
half_width = 2.0

VMEM = pl.BlockSpec(memory_space=pltpu.VMEM)
SMEM = pl.BlockSpec(memory_space=pltpu.SMEM)
PARAMS = pltpu.CompilerParams(vmem_limit_bytes=16 * 1024 * 1024)
f32 = jnp.float32
bf16 = jnp.bfloat16


def swap(value, axis, pattern):
    return lax.ppermute(value, axis, [(i, i ^ pattern) for i in range(lax.axis_size(axis))])


def local_call(kernel, shapes, *operands, specs=None, scratch=(), flops=1000, nbytes=100000, params=PARAMS):
    return pl.pallas_call(
        kernel,
        out_shape=[jax.ShapeDtypeStruct(s, d) for s, d in shapes],
        in_specs=specs or [VMEM] * len(operands),
        out_specs=[VMEM] * len(shapes),
        scratch_shapes=scratch,
        compiler_params=params,
        cost_estimate=pl.CostEstimate(flops=flops, bytes_accessed=nbytes, transcendentals=0),
    )(*operands)


def prepare(blocks, start_vecs, block_rows, block_cols, block_count):
    slots = blocks.shape[2]

    def kernel(count_ref, rows_hbm, cols_hbm, blocks_hbm, vecs_hbm, tiles_out, vecs_out, meta_out, rows_ref, cols_ref, sems):
        copies = [
            pltpu.make_async_copy(rows_hbm, rows_ref, sems.at[slots + 1]),
            pltpu.make_async_copy(cols_hbm, cols_ref, sems.at[slots + 2]),
        ]
        copies += [pltpu.make_async_copy(vecs_hbm, vecs_out, sems.at[slots])]
        copies += [pltpu.make_async_copy(blocks_hbm.at[0, 0, s], tiles_out.at[s], sems.at[s]) for s in range(slots)]
        for copy in copies:
            copy.start()
        row_at, col_at = lax.axis_index("row"), lax.axis_index("col")
        for copy in copies[:2]:
            copy.wait()
        count = count_ref[0, 0]
        for s in range(slots):
            meta_out[s] = jnp.where(s < count, rows_ref[0, 0, s] ^ row_at, 0)
            meta_out[slots + s] = jnp.where(s < count, cols_ref[0, 0, s] ^ col_at, 0)
        meta_out[2 * slots] = count
        for copy in copies[2:]:
            copy.wait()

    arrays = (block_rows, block_cols, blocks, start_vecs)
    return pl.pallas_call(
        kernel,
        out_shape=[
            pltpu.VMEM(blocks.shape[2:], blocks.dtype),
            pltpu.VMEM(start_vecs.shape, start_vecs.dtype),
            pltpu.SMEM((2 * slots + 1,), jnp.int32),
        ],
        in_specs=[SMEM] + [pl.BlockSpec(memory_space=pltpu.HBM)] * len(arrays),
        out_specs=[VMEM, VMEM, SMEM],
        scratch_shapes=[pltpu.SMEM(a.shape, a.dtype) for a in arrays[:2]] + [pltpu.SemaphoreType.DMA((slots + 3,))],
        compiler_params=PARAMS,
        cost_estimate=pl.CostEstimate(flops=1000, bytes_accessed=2 * blocks.size * 2, transcendentals=0),
    )(block_count, *[pltpu.with_memory_space_constraint(a, pltpu.HBM) for a in arrays])


def stacked(refs, n_vec):
    return [ref[k * n_vec : (k + 1) * n_vec, :] for ref in refs for k in range(ref.shape[0] // n_vec)]


def put(ref, k, value):
    n_vec = value.shape[0]
    ref[k * n_vec : (k + 1) * n_vec, :] = value.astype(ref.dtype)


def join(first, second, *after):
    rows = first.shape[0]

    def kernel(first_ref, second_ref, *refs):
        out_ref = refs[-1]
        out_ref[:rows, :] = first_ref[...]
        out_ref[rows:, :] = second_ref[...]

    return local_call(kernel, [((2 * rows, first.shape[1]), first.dtype)], first, second, *after)[0]


def gather(pair, at, axis, patterns):
    return [pair] + [swap(pair, axis, pattern) for pattern in patterns], at + [i ^ k for k in patterns for i in at]


def combinations(bits):
    found = [0]
    for bit in bits:
        found += [i | bit for i in found]
    return sorted(found, reverse=True)[:-1]


def shares(at, step):
    mask = 0
    for pattern in step:
        mask |= pattern
    mine = [i for i in at if not i & mask]
    return mine, [[i ^ pattern for i in mine] for pattern in step]


def total(refs, rows=slice(None)):
    value = refs[0][rows, :]
    for ref in refs[1:]:
        value = value + ref[rows, :].astype(f32)
    return value


def scatter(kept, sent, at, axis, steps):
    n_vec, width = kept.shape[0] // len(at), kept.shape[1]
    for step, following in zip(steps, steps[1:] + [None]):
        received = [swap(value, axis, pattern) for value, pattern in zip(sent, step, strict=True)]
        if following is None:
            return [kept, *received]
        mine, theirs = shares(at, following)
        order = at

        def kernel(kept_ref, *refs):
            ins, outs = refs[: len(received)], refs[len(received) :]
            totals = dict(zip(order, stacked([kept_ref], n_vec), strict=True))
            for ref in ins:
                for i, block in zip(order, stacked([ref], n_vec), strict=True):
                    totals[i] = totals[i] + block.astype(f32)
            for out, chosen in zip(outs, [*theirs, mine], strict=True):
                for n, i in enumerate(chosen):
                    put(out, n, totals[i])

        part = (len(mine) * n_vec, width)
        *sent, kept = local_call(kernel, [(part, bf16)] * len(theirs) + [(part, f32)], kept, *received)
        at = mine


def slot_products(meta, tiles, parts, at, targets, step, mirrored, after=()):
    slots, width = tiles.shape[0], tiles.shape[1]
    n_vec = sum(p.shape[0] for p in parts) // len(at)
    n_in = len(parts)
    mine, theirs = shares(list(range(targets)), step)

    def kernel(meta_ref, tiles_ref, *refs):
        ins, (*outs, vecs, totals) = refs[:n_in], refs[n_in + len(after) :]
        for i, block in zip(at, stacked(ins, n_vec), strict=True):
            vecs[i] = block
        totals[...] = jnp.zeros(totals.shape, f32)
        count = meta_ref[2 * slots]
        for s in range(slots):
            r, c = meta_ref[s], meta_ref[slots + s]
            source, target = (r, c) if mirrored else (c, r)
            values = jnp.where(s < count, vecs[source], jnp.zeros((), bf16))
            product = lax.dot_general(
                values, tiles_ref[s], (((1,), (0 if mirrored else 1,)), ((), ())), preferred_element_type=f32
            )
            totals[target] += product
        for out, chosen in zip(outs, [*theirs, mine], strict=True):
            for n, i in enumerate(chosen):
                put(out, n, totals[i])

    part = (len(mine) * n_vec, width)
    *sent, kept = local_call(
        kernel, [(part, bf16)] * len(theirs) + [(part, f32)], meta, tiles, *parts, *after,
        specs=[SMEM] + [VMEM] * (1 + n_in + len(after)),
        scratch=[pltpu.VMEM((len(at), n_vec, width), bf16), pltpu.VMEM((targets, n_vec, width), f32)],
        flops=slots * 2 * n_vec * width * width,
        nbytes=slots * width * width * 2,
    )
    return kept, sent, mine


def body(start_vecs, blocks, block_rows, block_cols, block_count):
    n_vec, width = start_vecs.shape[0], start_vecs.shape[4]
    n_row, n_col = lax.axis_size("row"), lax.axis_size("col")
    row_bits = [1 << k for k in range(n_row.bit_length() - 1)]
    col_bits = [1 << k for k in range(n_col.bit_length() - 1)]
    row_pair_bit, row_inner = row_bits[-1], combinations(row_bits[:-1])
    col_pair_bit, col_inner = col_bits[-1], combinations(col_bits[:-1])
    start = start_vecs.reshape(n_vec, width)
    tiles, start_here, meta = prepare(blocks, start, block_rows, block_cols, block_count)
    one, two = (n_vec, width), (2 * n_vec, width)
    low, high = slice(0, n_vec), slice(n_vec, 2 * n_vec)

    def products(row_pair, col_pair, row_steps, col_steps):
        parts, at = gather(row_pair, [0, row_pair_bit], "row", row_inner)
        mirror = slot_products(meta, tiles, parts, at, n_col, col_steps[0], True)
        parts, at = gather(col_pair, [0, col_pair_bit], "col", col_inner[::-1])
        direct = slot_products(meta, tiles, parts, at, n_row, row_steps[0], False, mirror[:1])
        return scatter(*direct, "row", row_steps), scatter(*mirror, "col", col_steps)

    def get(ref, rows):
        return ref[rows, :].astype(f32)

    start_y, start_z = swap(start, "row", row_pair_bit), swap(start, "col", col_pair_bit)
    d_terms, m_terms = products(join(start_here, start_y, start_z), join(start_here, start_z), [row_inner], [col_inner])

    n_d = len(d_terms)

    def partial_sums(*refs):
        *terms, to_diag, to_z, to_y, d_keep, m_keep = refs
        d_own, d_other = (total(terms[:n_d], rows) for rows in (low, high))
        m_own, m_other = (total(terms[n_d:], rows) for rows in (low, high))
        d_keep[low, :] = d_own
        d_keep[high, :] = d_other
        m_keep[low, :] = m_own
        m_keep[high, :] = m_other
        both = (d_own + m_own).astype(bf16)
        d_other, m_other = d_other.astype(bf16), m_other.astype(bf16)
        to_y[low, :] = d_other
        to_y[high, :] = both
        to_z[low, :] = m_other
        to_z[high, :] = both
        to_diag[low, :] = d_other
        to_diag[high, :] = m_other

    to_diag, to_z, to_y, d_sum, m_sum = local_call(
        partial_sums, [(two, bf16)] * 3 + [(two, f32)] * 2, *d_terms, *m_terms
    )
    diagonal = [
        (i * n_col + j, (i ^ row_pair_bit) * n_col + (j ^ col_pair_bit)) for i in range(n_row) for j in range(n_col)
    ]
    from_diag = lax.ppermute(to_diag, ("row", "col"), diagonal)
    from_z = swap(to_z, "col", col_pair_bit)
    from_y = swap(to_y, "row", row_pair_bit)

    def first_update(diag_ref, z_ref, y_ref, d_ref, m_ref, cur, cur_y, cur_z, row_out, col_out):
        def advance(applied, ref):
            shifted = (applied - shift_center * ref[...].astype(f32)) / half_width
            return shifted.astype(bf16)

        own = d_ref[low, :] + m_ref[low, :] + get(y_ref, low) + get(z_ref, low)
        own = advance(own, cur)
        row_out[low, :] = own
        col_out[low, :] = own
        row_out[high, :] = advance(d_ref[high, :] + get(y_ref, high) + get(diag_ref, high), cur_y)
        col_out[high, :] = advance(m_ref[high, :] + get(z_ref, high) + get(diag_ref, low), cur_z)

    row_pair, col_pair = local_call(
        first_update, [(two, bf16), (two, bf16)],
        from_diag, from_z, from_y, d_sum, m_sum, start_here, start_y, start_z,
    )
    d_terms, m_terms = products(row_pair, col_pair, [row_inner, [row_pair_bit]], [col_inner, [col_pair_bit]])
    n_last = len(d_terms)
    terms = [*d_terms, *m_terms]

    def last_update(*refs):
        *terms, pair_ref, prev_ref, first_out, second_out = refs
        current = pair_ref[low, :]
        applied = total(terms[:n_last]) + total(terms[n_last:])
        shifted = (applied - shift_center * current.astype(f32)) / half_width
        shifted = 2.0 * shifted - prev_ref[...].astype(f32)
        first_out[...] = current
        second_out[...] = shifted.astype(bf16)

    first, second = local_call(last_update, [(one, bf16), (one, bf16)], *terms, row_pair, start_here)
    shape = start_vecs.shape
    return first.reshape(shape), second.reshape(shape)


def solution(mesh):
    return jax.shard_map(
        body,
        mesh=mesh,
        in_specs=(
            P(None, None, "row", "col", None),
            P("row", "col", None, None, None),
            P("row", "col", None),
            P("row", "col", None),
            P("row", "col"),
        ),
        out_specs=(P(None, None, "row", "col", None), P(None, None, "row", "col", None)),
        check_vma=False,
    )
```

```python
import jax
import jax.numpy as jnp
from jax import lax
from jax.experimental import pallas as pl
from jax.experimental.pallas import tpu as pltpu
from jax.sharding import PartitionSpec as P

shift_center = 0.5
half_width = 2.0

VMEM = pl.BlockSpec(memory_space=pltpu.VMEM)
SMEM = pl.BlockSpec(memory_space=pltpu.SMEM)
PARAMS = pltpu.CompilerParams(vmem_limit_bytes=16 * 1024 * 1024)
f32 = jnp.float32
bf16 = jnp.bfloat16


def swap(value, axis, pattern):
    return lax.ppermute(value, axis, [(i, i ^ pattern) for i in range(lax.axis_size(axis))])


def local_call(kernel, shapes, *operands, specs=None, scratch=(), flops=1000, nbytes=100000, params=PARAMS):
    return pl.pallas_call(
        kernel,
        out_shape=[jax.ShapeDtypeStruct(s, d) for s, d in shapes],
        in_specs=specs or [VMEM] * len(operands),
        out_specs=[VMEM] * len(shapes),
        scratch_shapes=scratch,
        compiler_params=params,
        cost_estimate=pl.CostEstimate(flops=flops, bytes_accessed=nbytes, transcendentals=0),
    )(*operands)


def prepare(blocks, start_vecs, block_rows, block_cols, block_count):
    slots = blocks.shape[2]

    def kernel(count_ref, rows_hbm, cols_hbm, blocks_hbm, vecs_hbm, tiles_out, turned_out, vecs_out, meta_out, rows_ref, cols_ref, sems):
        copies = [
            pltpu.make_async_copy(rows_hbm, rows_ref, sems.at[slots + 1]),
            pltpu.make_async_copy(cols_hbm, cols_ref, sems.at[slots + 2]),
        ]
        copies += [pltpu.make_async_copy(vecs_hbm, vecs_out, sems.at[slots])]
        copies += [pltpu.make_async_copy(blocks_hbm.at[0, 0, s], tiles_out.at[s], sems.at[s]) for s in range(slots)]
        for copy in copies:
            copy.start()
        row_at, col_at = lax.axis_index("row"), lax.axis_index("col")
        for copy in copies[:2]:
            copy.wait()
        count = count_ref[0, 0]
        for s in range(slots):
            meta_out[s] = jnp.where(s < count, rows_ref[0, 0, s] ^ row_at, 0)
            meta_out[slots + s] = jnp.where(s < count, cols_ref[0, 0, s] ^ col_at, 0)
        meta_out[2 * slots] = count
        copies[2].wait()
        for s in range(slots):
            copies[3 + s].wait()
            turned_out[s] = tiles_out[s].T

    arrays = (block_rows, block_cols, blocks, start_vecs)
    return pl.pallas_call(
        kernel,
        out_shape=[
            pltpu.VMEM(blocks.shape[2:], blocks.dtype),
            pltpu.VMEM(blocks.shape[2:], blocks.dtype),
            pltpu.VMEM(start_vecs.shape, start_vecs.dtype),
            pltpu.SMEM((2 * slots + 1,), jnp.int32),
        ],
        in_specs=[SMEM] + [pl.BlockSpec(memory_space=pltpu.HBM)] * len(arrays),
        out_specs=[VMEM, VMEM, VMEM, SMEM],
        scratch_shapes=[pltpu.SMEM(a.shape, a.dtype) for a in arrays[:2]] + [pltpu.SemaphoreType.DMA((slots + 3,))],
        compiler_params=PARAMS,
        cost_estimate=pl.CostEstimate(flops=1000, bytes_accessed=2 * blocks.size * 2, transcendentals=0),
    )(block_count, *[pltpu.with_memory_space_constraint(a, pltpu.HBM) for a in arrays])


def stacked(refs, n_vec):
    return [ref[k * n_vec : (k + 1) * n_vec, :] for ref in refs for k in range(ref.shape[0] // n_vec)]


def put(ref, k, value):
    n_vec = value.shape[0]
    ref[k * n_vec : (k + 1) * n_vec, :] = value.astype(ref.dtype)


def join(first, second, *after):
    rows = first.shape[0]

    def kernel(first_ref, second_ref, *refs):
        out_ref = refs[-1]
        out_ref[:rows, :] = first_ref[...]
        out_ref[rows:, :] = second_ref[...]

    return local_call(kernel, [((2 * rows, first.shape[1]), first.dtype)], first, second, *after)[0]


def gather(pair, at, axis, patterns):
    return [pair] + [swap(pair, axis, pattern) for pattern in patterns], at + [i ^ k for k in patterns for i in at]


def combinations(bits):
    found = [0]
    for bit in bits:
        found += [i | bit for i in found]
    return sorted(found, reverse=True)[:-1]


def shares(at, step):
    mask = 0
    for pattern in step:
        mask |= pattern
    mine = [i for i in at if not i & mask]
    return mine, [[i ^ pattern for i in mine] for pattern in step]


def total(refs, rows=slice(None)):
    value = refs[0][rows, :]
    for ref in refs[1:]:
        value = value + ref[rows, :].astype(f32)
    return value


def scatter(kept, sent, at, axis, steps):
    n_vec, width = kept.shape[0] // len(at), kept.shape[1]
    for step, following in zip(steps, steps[1:] + [None]):
        received = [swap(value, axis, pattern) for value, pattern in zip(sent, step, strict=True)]
        if following is None:
            return [kept, *received]
        mine, theirs = shares(at, following)
        order = at

        def kernel(kept_ref, *refs):
            ins, outs = refs[: len(received)], refs[len(received) :]
            totals = dict(zip(order, stacked([kept_ref], n_vec), strict=True))
            for ref in ins:
                for i, block in zip(order, stacked([ref], n_vec), strict=True):
                    totals[i] = totals[i] + block.astype(f32)
            for out, chosen in zip(outs, [*theirs, mine], strict=True):
                for n, i in enumerate(chosen):
                    put(out, n, totals[i])

        part = (len(mine) * n_vec, width)
        *sent, kept = local_call(kernel, [(part, bf16)] * len(theirs) + [(part, f32)], kept, *received)
        at = mine


def slot_products(meta, tiles, parts, at, targets, step, mirrored, after=()):
    slots, width = tiles.shape[0], tiles.shape[1]
    n_vec = sum(p.shape[0] for p in parts) // len(at)
    n_in = len(parts)
    mine, theirs = shares(list(range(targets)), step)

    def kernel(meta_ref, tiles_ref, *refs):
        ins, (*outs, vecs, totals) = refs[:n_in], refs[n_in + len(after) :]
        for i, block in zip(at, stacked(ins, n_vec), strict=True):
            vecs[i] = block
        totals[...] = jnp.zeros(totals.shape, f32)
        count = meta_ref[2 * slots]
        for s in range(slots):
            r, c = meta_ref[s], meta_ref[slots + s]
            source, target = (r, c) if mirrored else (c, r)
            values = jnp.where(s < count, vecs[source], jnp.zeros((), bf16))
            product = jnp.dot(values, tiles_ref[s], preferred_element_type=f32)
            totals[target] += product
        for out, chosen in zip(outs, [*theirs, mine], strict=True):
            for n, i in enumerate(chosen):
                put(out, n, totals[i])

    part = (len(mine) * n_vec, width)
    *sent, kept = local_call(
        kernel, [(part, bf16)] * len(theirs) + [(part, f32)], meta, tiles, *parts, *after,
        specs=[SMEM] + [VMEM] * (1 + n_in + len(after)),
        scratch=[pltpu.VMEM((len(at), n_vec, width), bf16), pltpu.VMEM((targets, n_vec, width), f32)],
        flops=slots * 2 * n_vec * width * width,
        nbytes=slots * width * width * 2,
    )
    return kept, sent, mine


def body(start_vecs, blocks, block_rows, block_cols, block_count):
    n_vec, width = start_vecs.shape[0], start_vecs.shape[4]
    n_row, n_col = lax.axis_size("row"), lax.axis_size("col")
    row_bits = [1 << k for k in range(n_row.bit_length() - 1)]
    col_bits = [1 << k for k in range(n_col.bit_length() - 1)]
    row_pair_bit, row_inner = row_bits[-1], combinations(row_bits[:-1])
    col_pair_bit, col_inner = col_bits[-1], combinations(col_bits[:-1])
    start = start_vecs.reshape(n_vec, width)
    tiles, turned, start_here, meta = prepare(blocks, start, block_rows, block_cols, block_count)
    one, two = (n_vec, width), (2 * n_vec, width)
    low, high = slice(0, n_vec), slice(n_vec, 2 * n_vec)

    def products(row_pair, col_pair, row_steps, col_steps):
        parts, at = gather(row_pair, [0, row_pair_bit], "row", row_inner)
        mirror = slot_products(meta, tiles, parts, at, n_col, col_steps[0], True)
        parts, at = gather(col_pair, [0, col_pair_bit], "col", col_inner[::-1])
        direct = slot_products(meta, turned, parts, at, n_row, row_steps[0], False, mirror[:1])
        return scatter(*direct, "row", row_steps), scatter(*mirror, "col", col_steps)

    def get(ref, rows):
        return ref[rows, :].astype(f32)

    start_y, start_z = swap(start, "row", row_pair_bit), swap(start, "col", col_pair_bit)
    d_terms, m_terms = products(join(start_here, start_y), join(start_here, start_z), [row_inner], [col_inner])

    n_d = len(d_terms)

    def partial_sums(*refs):
        *terms, to_diag, to_z, to_y, d_keep, m_keep = refs
        d_own, d_other = (total(terms[:n_d], rows) for rows in (low, high))
        m_own, m_other = (total(terms[n_d:], rows) for rows in (low, high))
        d_keep[low, :] = d_own
        d_keep[high, :] = d_other
        m_keep[low, :] = m_own
        m_keep[high, :] = m_other
        both = (d_own + m_own).astype(bf16)
        d_other, m_other = d_other.astype(bf16), m_other.astype(bf16)
        to_y[low, :] = d_other
        to_y[high, :] = both
        to_z[low, :] = m_other
        to_z[high, :] = both
        to_diag[low, :] = d_other
        to_diag[high, :] = m_other

    to_diag, to_z, to_y, d_sum, m_sum = local_call(
        partial_sums, [(two, bf16)] * 3 + [(two, f32)] * 2, *d_terms, *m_terms
    )
    diagonal = [
        (i * n_col + j, (i ^ row_pair_bit) * n_col + (j ^ col_pair_bit)) for i in range(n_row) for j in range(n_col)
    ]
    from_diag = lax.ppermute(to_diag, ("row", "col"), diagonal)
    from_z = swap(to_z, "col", col_pair_bit)
    from_y = swap(to_y, "row", row_pair_bit)

    def first_update(diag_ref, z_ref, y_ref, d_ref, m_ref, cur, cur_y, cur_z, row_out, col_out):
        def advance(applied, ref):
            shifted = (applied - shift_center * ref[...].astype(f32)) / half_width
            return shifted.astype(bf16)

        own = d_ref[low, :] + m_ref[low, :] + get(y_ref, low) + get(z_ref, low)
        own = advance(own, cur)
        row_out[low, :] = own
        col_out[low, :] = own
        row_out[high, :] = advance(d_ref[high, :] + get(y_ref, high) + get(diag_ref, high), cur_y)
        col_out[high, :] = advance(m_ref[high, :] + get(z_ref, high) + get(diag_ref, low), cur_z)

    row_pair, col_pair = local_call(
        first_update, [(two, bf16), (two, bf16)],
        from_diag, from_z, from_y, d_sum, m_sum, start_here, start_y, start_z,
    )
    d_terms, m_terms = products(row_pair, col_pair, [[row_pair_bit], row_inner], [col_inner, [col_pair_bit]])
    n_last = len(d_terms)
    terms = [*d_terms, *m_terms]

    def last_update(*refs):
        *terms, pair_ref, prev_ref, first_out, second_out = refs
        current = pair_ref[low, :]
        applied = total(terms[:n_last]) + total(terms[n_last:])
        shifted = (applied - shift_center * current.astype(f32)) / half_width
        shifted = 2.0 * shifted - prev_ref[...].astype(f32)
        first_out[...] = current
        second_out[...] = shifted.astype(bf16)

    first, second = local_call(last_update, [(one, bf16), (one, bf16)], *terms, row_pair, start_here)
    shape = start_vecs.shape
    return first.reshape(shape), second.reshape(shape)


def solution(mesh):
    return jax.shard_map(
        body,
        mesh=mesh,
        in_specs=(
            P(None, None, "row", "col", None),
            P("row", "col", None, None, None),
            P("row", "col", None),
            P("row", "col", None),
            P("row", "col"),
        ),
        out_specs=(P(None, None, "row", "col", None), P(None, None, "row", "col", None)),
        check_vma=False,
    )
```

```python
import jax
import jax.numpy as jnp
from jax import lax
from jax.experimental import pallas as pl
from jax.experimental.pallas import tpu as pltpu
from jax.sharding import PartitionSpec as P

shift_center = 0.5
half_width = 2.0

VMEM = pl.BlockSpec(memory_space=pltpu.VMEM)
SMEM = pl.BlockSpec(memory_space=pltpu.SMEM)
PARAMS = pltpu.CompilerParams(vmem_limit_bytes=16 * 1024 * 1024)
f32 = jnp.float32
bf16 = jnp.bfloat16


def swap(value, axis, pattern):
    return lax.ppermute(value, axis, [(i, i ^ pattern) for i in range(lax.axis_size(axis))])


def local_call(kernel, shapes, *operands, specs=None, scratch=(), flops=1000, nbytes=100000, params=PARAMS):
    return pl.pallas_call(
        kernel,
        out_shape=[jax.ShapeDtypeStruct(s, d) for s, d in shapes],
        in_specs=specs or [VMEM] * len(operands),
        out_specs=[VMEM] * len(shapes),
        scratch_shapes=scratch,
        compiler_params=params,
        cost_estimate=pl.CostEstimate(flops=flops, bytes_accessed=nbytes, transcendentals=0),
    )(*operands)


def prepare(blocks, start_vecs, block_rows, block_cols, block_count):
    slots = blocks.shape[2]

    def kernel(count_ref, rows_hbm, cols_hbm, blocks_hbm, vecs_hbm, tiles_out, turned_out, vecs_out, meta_out, rows_ref, cols_ref, sems):
        copies = [
            pltpu.make_async_copy(rows_hbm, rows_ref, sems.at[slots + 1]),
            pltpu.make_async_copy(cols_hbm, cols_ref, sems.at[slots + 2]),
        ]
        copies += [pltpu.make_async_copy(vecs_hbm, vecs_out, sems.at[slots])]
        copies += [pltpu.make_async_copy(blocks_hbm.at[0, 0, s], tiles_out.at[s], sems.at[s]) for s in range(slots)]
        for copy in copies:
            copy.start()
        row_at, col_at = lax.axis_index("row"), lax.axis_index("col")
        for copy in copies[:2]:
            copy.wait()
        count = count_ref[0, 0]
        for s in range(slots):
            meta_out[s] = jnp.where(s < count, rows_ref[0, 0, s] ^ row_at, 0)
            meta_out[slots + s] = jnp.where(s < count, cols_ref[0, 0, s] ^ col_at, 0)
        meta_out[2 * slots] = count
        copies[2].wait()
        for s in range(slots):
            copies[3 + s].wait()
            turned_out[s] = tiles_out[s].T

    arrays = (block_rows, block_cols, blocks, start_vecs)
    return pl.pallas_call(
        kernel,
        out_shape=[
            pltpu.VMEM(blocks.shape[2:], blocks.dtype),
            pltpu.VMEM(blocks.shape[2:], blocks.dtype),
            pltpu.VMEM(start_vecs.shape, start_vecs.dtype),
            pltpu.SMEM((2 * slots + 1,), jnp.int32),
        ],
        in_specs=[SMEM] + [pl.BlockSpec(memory_space=pltpu.HBM)] * len(arrays),
        out_specs=[VMEM, VMEM, VMEM, SMEM],
        scratch_shapes=[pltpu.SMEM(a.shape, a.dtype) for a in arrays[:2]] + [pltpu.SemaphoreType.DMA((slots + 3,))],
        compiler_params=PARAMS,
        cost_estimate=pl.CostEstimate(flops=1000, bytes_accessed=2 * blocks.size * 2, transcendentals=0),
    )(block_count, *[pltpu.with_memory_space_constraint(a, pltpu.HBM) for a in arrays])


def stacked(refs, n_vec):
    return [ref[k * n_vec : (k + 1) * n_vec, :] for ref in refs for k in range(ref.shape[0] // n_vec)]


def put(ref, k, value):
    n_vec = value.shape[0]
    ref[k * n_vec : (k + 1) * n_vec, :] = value.astype(ref.dtype)


def join(first, second, *after):
    rows = first.shape[0]

    def kernel(first_ref, second_ref, *refs):
        out_ref = refs[-1]
        out_ref[:rows, :] = first_ref[...]
        out_ref[rows:, :] = second_ref[...]

    return local_call(kernel, [((2 * rows, first.shape[1]), first.dtype)], first, second, *after)[0]


def gather(pair, at, axis, patterns):
    return [pair] + [swap(pair, axis, pattern) for pattern in patterns], at + [i ^ k for k in patterns for i in at]


def combinations(bits):
    found = [0]
    for bit in bits:
        found += [i | bit for i in found]
    return sorted(found, reverse=True)[:-1]


def shares(at, step):
    mask = 0
    for pattern in step:
        mask |= pattern
    mine = [i for i in at if not i & mask]
    return mine, [[i ^ pattern for i in mine] for pattern in step]


def total(refs, rows=slice(None)):
    value = refs[0][rows, :]
    for ref in refs[1:]:
        value = value + ref[rows, :].astype(f32)
    return value


def scatter(kept, sent, at, axis, steps):
    n_vec, width = kept.shape[0] // len(at), kept.shape[1]
    for step, following in zip(steps, steps[1:] + [None]):
        received = [swap(value, axis, pattern) for value, pattern in zip(sent, step, strict=True)]
        if following is None:
            return [kept, *received]
        mine, theirs = shares(at, following)
        order = at

        def kernel(kept_ref, *refs):
            ins, outs = refs[: len(received)], refs[len(received) :]
            totals = dict(zip(order, stacked([kept_ref], n_vec), strict=True))
            for ref in ins:
                for i, block in zip(order, stacked([ref], n_vec), strict=True):
                    totals[i] = totals[i] + block.astype(f32)
            for out, chosen in zip(outs, [*theirs, mine], strict=True):
                for n, i in enumerate(chosen):
                    put(out, n, totals[i])

        part = (len(mine) * n_vec, width)
        *sent, kept = local_call(kernel, [(part, bf16)] * len(theirs) + [(part, f32)], kept, *received)
        at = mine


def slot_products(meta, tiles, parts, at, targets, step, mirrored, after=()):
    slots, width = tiles.shape[0], tiles.shape[1]
    n_vec = sum(p.shape[0] for p in parts) // len(at)
    n_in = len(parts)
    mine, theirs = shares(list(range(targets)), step)

    def kernel(meta_ref, tiles_ref, *refs):
        ins, (*outs, vecs, totals) = refs[:n_in], refs[n_in + len(after) :]
        for i, block in zip(at, stacked(ins, n_vec), strict=True):
            vecs[i] = block
        totals[...] = jnp.zeros(totals.shape, f32)
        count = meta_ref[2 * slots]
        for s in range(slots):
            r, c = meta_ref[s], meta_ref[slots + s]
            source, target = (r, c) if mirrored else (c, r)
            values = jnp.where(s < count, vecs[source], jnp.zeros((), bf16))
            product = jnp.dot(values, tiles_ref[s], preferred_element_type=f32)
            totals[target] += product
        for out, chosen in zip(outs, [*theirs, mine], strict=True):
            for n, i in enumerate(chosen):
                put(out, n, totals[i])

    part = (len(mine) * n_vec, width)
    *sent, kept = local_call(
        kernel, [(part, bf16)] * len(theirs) + [(part, f32)], meta, tiles, *parts, *after,
        specs=[SMEM] + [VMEM] * (1 + n_in + len(after)),
        scratch=[pltpu.VMEM((len(at), n_vec, width), bf16), pltpu.VMEM((targets, n_vec, width), f32)],
        flops=slots * 2 * n_vec * width * width,
        nbytes=slots * width * width * 2,
    )
    return kept, sent, mine


def body(start_vecs, blocks, block_rows, block_cols, block_count):
    n_vec, width = start_vecs.shape[0], start_vecs.shape[4]
    n_row, n_col = lax.axis_size("row"), lax.axis_size("col")
    row_bits = [1 << k for k in range(n_row.bit_length() - 1)]
    col_bits = [1 << k for k in range(n_col.bit_length() - 1)]
    row_pair_bit, row_inner = row_bits[-1], combinations(row_bits[:-1])
    col_pair_bit, col_inner = col_bits[-1], combinations(col_bits[:-1])
    col_scatter = col_inner[:1] + col_inner[:0:-1]
    start = start_vecs.reshape(n_vec, width)
    tiles, turned, start_here, meta = prepare(blocks, start, block_rows, block_cols, block_count)
    one, two = (n_vec, width), (2 * n_vec, width)
    low, high = slice(0, n_vec), slice(n_vec, 2 * n_vec)

    def products(row_pair, col_pair, row_steps, col_steps):
        parts, at = gather(row_pair, [0, row_pair_bit], "row", row_inner)
        mirror = slot_products(meta, tiles, parts, at, n_col, col_steps[0], True)
        parts, at = gather(col_pair, [0, col_pair_bit], "col", col_inner[::-1])
        direct = slot_products(meta, turned, parts, at, n_row, row_steps[0], False, mirror[:1])
        return scatter(*direct, "row", row_steps), scatter(*mirror, "col", col_steps)

    def get(ref, rows):
        return ref[rows, :].astype(f32)

    start_y, start_z = swap(start, "row", row_pair_bit), swap(start, "col", col_pair_bit)
    d_terms, m_terms = products(join(start_here, start_y), join(start_here, start_z), [row_inner], [col_scatter])

    n_d = len(d_terms)

    def partial_sums(*refs):
        *terms, to_diag, to_z, to_y, d_keep, m_keep = refs
        d_own, d_other = (total(terms[:n_d], rows) for rows in (low, high))
        m_own, m_other = (total(terms[n_d:], rows) for rows in (low, high))
        d_keep[low, :] = d_own
        d_keep[high, :] = d_other
        m_keep[low, :] = m_own
        m_keep[high, :] = m_other
        both = (d_own + m_own).astype(bf16)
        d_other, m_other = d_other.astype(bf16), m_other.astype(bf16)
        to_y[low, :] = d_other
        to_y[high, :] = both
        to_z[low, :] = m_other
        to_z[high, :] = both
        to_diag[low, :] = d_other
        to_diag[high, :] = m_other

    to_diag, to_z, to_y, d_sum, m_sum = local_call(
        partial_sums, [(two, bf16)] * 3 + [(two, f32)] * 2, *d_terms, *m_terms
    )
    diagonal = [
        (i * n_col + j, (i ^ row_pair_bit) * n_col + (j ^ col_pair_bit)) for i in range(n_row) for j in range(n_col)
    ]
    from_diag = lax.ppermute(to_diag, ("row", "col"), diagonal)
    from_z = swap(to_z, "col", col_pair_bit)
    from_y = swap(to_y, "row", row_pair_bit)

    def first_update(diag_ref, z_ref, y_ref, d_ref, m_ref, cur, cur_y, cur_z, row_out, col_out):
        def advance(applied, ref):
            shifted = (applied - shift_center * ref[...].astype(f32)) / half_width
            return shifted.astype(bf16)

        own = d_ref[low, :] + m_ref[low, :] + get(y_ref, low) + get(z_ref, low)
        own = advance(own, cur)
        row_out[low, :] = own
        col_out[low, :] = own
        row_out[high, :] = advance(d_ref[high, :] + get(y_ref, high) + get(diag_ref, high), cur_y)
        col_out[high, :] = advance(m_ref[high, :] + get(z_ref, high) + get(diag_ref, low), cur_z)

    row_pair, col_pair = local_call(
        first_update, [(two, bf16), (two, bf16)],
        from_diag, from_z, from_y, d_sum, m_sum, start_here, start_y, start_z,
    )
    d_terms, m_terms = products(row_pair, col_pair, [[row_pair_bit], row_inner], [col_scatter, [col_pair_bit]])
    n_last = len(d_terms)
    terms = [*d_terms, *m_terms]

    def last_update(*refs):
        *terms, pair_ref, prev_ref, first_out, second_out = refs
        current = pair_ref[low, :]
        applied = total(terms[:n_last]) + total(terms[n_last:])
        shifted = (applied - shift_center * current.astype(f32)) / half_width
        shifted = 2.0 * shifted - prev_ref[...].astype(f32)
        first_out[...] = current
        second_out[...] = shifted.astype(bf16)

    first, second = local_call(last_update, [(one, bf16), (one, bf16)], *terms, row_pair, start_here)
    shape = start_vecs.shape
    return first.reshape(shape), second.reshape(shape)


def solution(mesh):
    return jax.shard_map(
        body,
        mesh=mesh,
        in_specs=(
            P(None, None, "row", "col", None),
            P("row", "col", None, None, None),
            P("row", "col", None),
            P("row", "col", None),
            P("row", "col"),
        ),
        out_specs=(P(None, None, "row", "col", None), P(None, None, "row", "col", None)),
        check_vma=False,
    )
```
